512 devices in a mesh: row: 16 (over z, x_hi), col: 32 (over y, x_lo, core).
Axes of the slice: x: 4 (x_hi: 2, x_lo: 2; x = x_hi * 2 + x_lo), y: 8, z: 8, core: 2. Of those that a mesh axis runs over, the one named last changes fastest.
Arguments:
- tokens: bfloat16 [1024, 8192], P('col', 'row'), may hold values from -6 to 6
- out_grad: bfloat16 [1024, 8192], P('col', 'row'), may hold values from -4 to 4
- gate_weight: bfloat16 [8192, 16384], P('row', 'col'), may hold values from -0.0625 to 0.0625
- up_weight: bfloat16 [8192, 16384], P('row', 'col'), may hold values from -0.0625 to 0.0625
- down_weight: bfloat16 [16384, 8192], P('col', 'row'), may hold values from -0.046875 to 0.046875
Outputs:
- in_grad: bfloat16 [1024, 8192], P('col', 'row')
- gate_wgrad: bfloat16 [8192, 16384], P('row', 'col')
- up_wgrad: bfloat16 [8192, 16384], P('row', 'col')
- down_wgrad: bfloat16 [16384, 8192], P('col', 'row')
The draws below stay inside these ranges and needn't reach their ends.
All inputs are finite; a program needn't handle non-finite values.
Results may differ from the reference program's by a relative error of at most 0.0049.
Values may be sent and summed in bfloat16 or wider, within the bound.
No kernel may reach another device: no remote copies, remote signals or barrier semaphores. Data moves between devices by JAX's collectives and lax.ppermute only.
A program may use at most 64 MiB of HBM per device.

```python
import jax
import jax.numpy as jnp
from jax import lax

D = 8192
FF = 16384
TOKENS = 1024


def block_scale(rng, dims, cuts, smallest, top_value):
    def one(axis_at, shards_of):
        draws = jax.random.uniform(jax.random.fold_in(jax.random.fold_in(rng, 6), axis_at), (shards_of,), jnp.float32, smallest / len(cuts), top_value / len(cuts))
        return jnp.repeat(jnp.exp(draws), dims[axis_at] // shards_of).reshape((-1,) + (1,) * (len(dims) - axis_at - 1))

    gain = one(*cuts[0])
    for cut in cuts[1:]:
        gain = gain * one(*cut)
    return gain


def centred(own_key, shape, width, bound, shards=(), held_as=jnp.bfloat16):
    array = width * jax.random.normal(own_key, shape, jnp.float32)
    if shards:
        array = array * block_scale(own_key, shape, shards, -0.22, 0.18)
    return jnp.clip(array, -bound, bound).astype(held_as)


def setup_inputs(seed: int = 0) -> dict:
    streams_of = jax.random.split(jax.random.key(seed), 6)
    return {
        "tokens": centred(streams_of[0], (TOKENS, D), 1.0, 6.0, ((0, 32), (1, 16))),
        "out_grad": centred(streams_of[1], (TOKENS, D), 0.25, 4.0, ((0, 32), (1, 16))),
        "gate_weight": centred(streams_of[2], (D, FF), D ** -0.5, 0.0625, ((0, 16), (1, 32))),
        "up_weight": centred(streams_of[3], (D, FF), D ** -0.5, 0.0625, ((0, 16), (1, 32))),
        "down_weight": centred(streams_of[4], (FF, D), FF ** -0.5, 0.046875, ((0, 32), (1, 16))),
    }


def swiglu_back(gate, up, hidden_grad):
    sig = jax.nn.sigmoid(gate)
    act = gate * sig
    hidden = (act * up).astype(jnp.bfloat16)
    gate_grad = (hidden_grad * up * sig * (1.0 + gate * (1.0 - sig))).astype(jnp.bfloat16)
    up_grad = (hidden_grad * act).astype(jnp.bfloat16)
    return hidden, gate_grad, up_grad


def reference(tokens, out_grad, gate_weight, up_weight, down_weight):
    gate = jnp.dot(tokens, gate_weight, preferred_element_type=jnp.float32)
    up = jnp.dot(tokens, up_weight, preferred_element_type=jnp.float32)
    hidden_grad = lax.dot_general(out_grad, down_weight, (((1,), (1,)), ((), ())), preferred_element_type=jnp.float32)
    hidden, gate_grad, up_grad = swiglu_back(gate, up, hidden_grad)
    down_wgrad = lax.dot_general(hidden, out_grad, (((0,), (0,)), ((), ())), preferred_element_type=jnp.float32).astype(jnp.bfloat16)
    gate_wgrad = lax.dot_general(tokens, gate_grad, (((0,), (0,)), ((), ())), preferred_element_type=jnp.float32).astype(jnp.bfloat16)
    up_wgrad = lax.dot_general(tokens, up_grad, (((0,), (0,)), ((), ())), preferred_element_type=jnp.float32).astype(jnp.bfloat16)
    back = lax.dot_general(gate_grad, gate_weight, (((1,), (1,)), ((), ())), preferred_element_type=jnp.float32)
    back = back + lax.dot_general(up_grad, up_weight, (((1,), (1,)), ((), ())), preferred_element_type=jnp.float32)
    return back.astype(jnp.bfloat16), gate_wgrad, up_wgrad, down_wgrad
```

```python
import jax
import jax.numpy as jnp
from jax import lax
from jax.sharding import Mesh, PartitionSpec as P

ROW = ("zh", "zl", "xh")
COL = ("y", "xl", "c")
WEIGHT_BOUND = 0.0625
DOWN_BOUND = 0.046875


def swiglu_back(gate, up, hidden_grad):
    sig = jax.nn.sigmoid(gate)
    act = gate * sig
    hidden = (act * up).astype(jnp.bfloat16)
    gate_grad = (hidden_grad * up * sig * (1.0 + gate * (1.0 - sig))).astype(jnp.bfloat16)
    up_grad = (hidden_grad * act).astype(jnp.bfloat16)
    return (hidden, gate_grad, up_grad)


def contract_rows(left, right):
    return lax.dot_general(
        left, right, (((0,), (0,)), ((), ())), preferred_element_type=jnp.float32
    )


def contract_cols(left, right):
    return lax.dot_general(
        left, right, (((1,), (1,)), ((), ())), preferred_element_type=jnp.float32
    )


def matmul(left, right):
    return jnp.dot(left, right, preferred_element_type=jnp.float32)


def swap(x, axis):
    return lax.ppermute(x, axis, [(0, 1), (1, 0)])


def scale_exponent(x, weight_bound, depth):
    top = jnp.max(jnp.abs(x)).astype(jnp.float32)
    bound = jnp.maximum(top, 1e-30) * (weight_bound * depth)
    return jnp.clip(jnp.floor(14.0 - jnp.log2(bound)), -100.0, 100.0)


def per_device(zh_size, blocks, tokens, out_grad, gate_weight, up_weight, down_weight):
    zl = lax.axis_index("zl")
    xh = lax.axis_index("xh")
    rows, depth = tokens.shape
    ff = gate_weight.shape[1]

    near = jnp.concatenate([gate_weight, up_weight, down_weight], axis=0)
    far = swap(near, "zl")
    far_gate, far_up, far_down = far[:depth], far[depth : 2 * depth], far[2 * depth :]

    shard = jnp.concatenate([tokens, out_grad], axis=1)
    own = lax.all_to_all(
        jnp.broadcast_to(shard[None], (blocks, rows, 2 * depth)), ("y", "xl"), 0, 0, tiled=True
    )
    own = own.reshape(zh_size // 2, 2, -1, 2 * depth)
    first = zl == 0
    mine = jnp.where(first, own[:, 0], own[:, 1])
    theirs = jnp.where(first, own[:, 1], own[:, 0])
    ext = swap(theirs, "zl").reshape(-1, 2 * depth)
    own = own.reshape(-1, 2 * depth)
    other = swap(own, "c")
    ext_other = swap(ext, "c")
    other_halves = other.reshape(zh_size // 2, 2, -1, 2 * depth)
    mine_other = jnp.where(first, other_halves[:, 0], other_halves[:, 1])
    every = jnp.concatenate([own, other], axis=0)
    near_half = jnp.concatenate([mine, mine_other], axis=0).reshape(-1, 2 * depth)
    far_half = jnp.concatenate([ext, ext_other], axis=0)
    inputs, grads = every[:, :depth], every[:, depth:]

    gate_part = matmul(near_half[:, :depth], gate_weight) + matmul(far_half[:, :depth], far_gate)
    up_part = matmul(near_half[:, :depth], up_weight) + matmul(far_half[:, :depth], far_up)
    hidden_part = contract_cols(near_half[:, depth:], down_weight) + contract_cols(
        far_half[:, depth:], far_down
    )

    both = jnp.concatenate([near_half, far_half], axis=1).reshape(-1, 2, 2, depth)
    exp_in = scale_exponent(both[:, :, 0], WEIGHT_BOUND, 2 * depth)
    exp_grad = scale_exponent(both[:, :, 1], DOWN_BOUND, 2 * depth)
    half = near_half.shape[0]
    parts = jnp.concatenate(
        [
            gate_part * jnp.exp2(exp_in),
            up_part * jnp.exp2(exp_in),
            hidden_part * jnp.exp2(exp_grad),
            jnp.full((half, 64), exp_in, jnp.float32),
            jnp.full((half, 64), exp_grad, jnp.float32),
        ],
        axis=1,
    ).astype(jnp.float16)
    group = 2 * zh_size
    parts = parts.reshape(group, half // group, -1)
    parts = lax.all_to_all(parts, ("zh", "xh"), 0, 0, tiled=True).astype(jnp.float32)
    in_scale = jnp.exp2(-parts[:, :1, 3 * ff : 3 * ff + 1])
    grad_scale = jnp.exp2(-parts[:, :1, 3 * ff + 64 : 3 * ff + 65])
    gate = jnp.sum(parts[:, :, :ff] * in_scale, axis=0)
    up = jnp.sum(parts[:, :, ff : 2 * ff] * in_scale, axis=0)
    hidden_grad = jnp.sum(parts[:, :, 2 * ff : 3 * ff] * grad_scale, axis=0)
    trio = jnp.concatenate(swiglu_back(gate, up, hidden_grad), axis=1)

    beside = swap(trio, "xh")
    pair = jnp.concatenate(
        [jnp.where(xh == 0, trio, beside), jnp.where(xh == 0, beside, trio)], axis=0
    )
    trio = lax.all_gather(pair, ("zh", "zl"), axis=0, tiled=True)
    hidden, gate_grad, up_grad = trio[:, :ff], trio[:, ff : 2 * ff], trio[:, 2 * ff :]

    in_part = contract_cols(gate_grad, gate_weight) + contract_cols(up_grad, up_weight)
    share = in_part.shape[0] // 2
    in_part = in_part[:share] + swap(in_part[share:], "c")
    in_part = lax.all_to_all(
        in_part.astype(jnp.bfloat16).reshape(blocks, rows, depth), ("y", "xl"), 0, 0, tiled=True
    )
    in_grad = jnp.sum(in_part.astype(jnp.float32), axis=0).astype(jnp.bfloat16)

    down_wgrad = contract_rows(hidden, grads).astype(jnp.bfloat16)
    gate_wgrad = contract_rows(inputs, gate_grad).astype(jnp.bfloat16)
    up_wgrad = contract_rows(inputs, up_grad).astype(jnp.bfloat16)
    return (in_grad, gate_wgrad, up_wgrad, down_wgrad)


def solution(mesh):
    row, col = mesh.devices.shape
    zh_size, y_size = row // 4, col // 4
    fine = Mesh(
        mesh.devices.reshape(zh_size, 2, 2, y_size, 2, 2), ("zh", "zl", "xh", "y", "xl", "c")
    )

    def body(*args):
        return per_device(zh_size, 2 * y_size, *args)

    in_specs = (P(COL, ROW), P(COL, ROW), P(ROW, COL), P(ROW, COL), P(COL, ROW))
    out_specs = (P(COL, ROW), P(ROW, COL), P(ROW, COL), P(COL, ROW))
    return jax.shard_map(
        body, mesh=fine, in_specs=in_specs, out_specs=out_specs, check_vma=False
    )
```

```python
import functools

import jax
import jax.numpy as jnp
from jax import lax
from jax.experimental import pallas as pl
from jax.experimental.pallas import tpu as pltpu
from jax.sharding import Mesh, PartitionSpec as P

ROW = ("zh", "zl", "xh")
COL = ("y", "xl", "c")
LANES = 128
TAIL = 16


def swiglu_back(gate, up, hidden_grad):
    sig = jax.nn.sigmoid(gate)
    act = gate * sig
    hidden = (act * up).astype(jnp.bfloat16)
    gate_grad = (hidden_grad * up * sig * (1.0 + gate * (1.0 - sig))).astype(jnp.bfloat16)
    up_grad = (hidden_grad * act).astype(jnp.bfloat16)
    return (hidden, gate_grad, up_grad)


def contract_rows(left, right):
    return lax.dot_general(
        left, right, (((0,), (0,)), ((), ())), preferred_element_type=jnp.float32
    )


def contract_cols(left, right):
    return lax.dot_general(
        left, right, (((1,), (1,)), ((), ())), preferred_element_type=jnp.float32
    )


def matmul(left, right):
    return jnp.dot(left, right, preferred_element_type=jnp.float32)


def swap(x, axis):
    return lax.ppermute(x, axis, [(0, 1), (1, 0)])


def forward_kernel(half_ref, own, other, ext, ext_other, gate_w, up_w, down_w, far, out):
    half = half_ref[0]
    depth = gate_w.shape[0]
    near = [source[i, half] for source in (own, other) for i in range(own.shape[0])]
    near = jnp.concatenate(near, axis=0)
    beyond = jnp.concatenate([ext[...], ext_other[...]], axis=0)
    group, rows = out.shape[0], near.shape[0] // out.shape[0]
    lane_blocks = gate_w.shape[1] // LANES
    place = lax.broadcasted_iota(jnp.int32, (TAIL, LANES), 0)
    tail = jnp.zeros((TAIL, LANES), jnp.float32)
    for n in range(3):
        far_w = far[n * depth : (n + 1) * depth, :]
        if n == 2:
            part = contract_cols(near[:, depth:], down_w[...]) + contract_cols(
                beyond[:, depth:], far_w
            )
        else:
            near_w = (gate_w, up_w)[n][...]
            part = matmul(near[:, :depth], near_w) + matmul(beyond[:, :depth], far_w)
        top = jnp.max(jnp.abs(part), axis=0, keepdims=True)
        top = jnp.max(top, axis=1, keepdims=True)
        exponent = jnp.floor(14.0 - jnp.log2(jnp.maximum(top, 1e-30)))
        exponent = jnp.clip(exponent, -100.0, 100.0)
        part = part * jnp.exp2(exponent)
        for j in range(group):
            for q in range(lane_blocks):
                at = (n * lane_blocks + q) * rows
                out[j, at : at + rows, :] = part[
                    j * rows : (j + 1) * rows, q * LANES : (q + 1) * LANES
                ]
        tail = jnp.where(place == n, exponent, tail)
    for j in range(group):
        out[j, 3 * lane_blocks * rows :, :] = tail


def middle_kernel(parts, trio):
    rows, ff = trio.shape[0], trio.shape[1] // 3
    lane_blocks = ff // LANES
    tail = 3 * lane_blocks * rows
    scales = [jnp.exp2(-parts[:, tail + n : tail + n + 1, :]) for n in range(3)]
    for q in range(lane_blocks):
        sums = []
        for n in range(3):
            at = (n * lane_blocks + q) * rows
            sums.append(jnp.sum(parts[:, at : at + rows, :] * scales[n], axis=0))
        for n, value in enumerate(swiglu_back(*sums)):
            at = n * ff + q * LANES
            trio[:, at : at + LANES] = value


def backward_kernel(zh_size, place, gate_w, up_w, trio_in, *refs):
    size = 2 * zh_size
    rights, refs = refs[:zh_size], refs[zh_size:]
    lefts, refs = refs[: zh_size - 1], refs[zh_size - 1 :]
    beside, (trio, in_own, in_other) = refs[: zh_size + 1], refs[zh_size + 1 :]
    rows, ff = trio_in.shape[0], gate_w.shape[1]
    z, xh = place[0], place[1]

    def put(distance, mine, others):
        at = 2 * rows * lax.rem(z + distance + size, size)
        trio[pl.ds(pl.multiple_of(at + rows * xh, rows), rows), :] = mine
        trio[pl.ds(pl.multiple_of(at + rows * (1 - xh), rows), rows), :] = others

    put(0, trio_in[...], beside[0][...])
    for k in range(1, zh_size):
        put(-k, rights[k - 1][...], beside[k][:rows, :])
        put(k, lefts[k - 1][...], beside[k][rows:, :])
    put(-zh_size, rights[-1][...], beside[-1][...])
    share = in_own.shape[0]
    for part, target in ((1, in_other), (0, in_own)):
        at = slice(part * share, (part + 1) * share)
        target[...] = contract_cols(trio[at, ff : 2 * ff], gate_w[...]) + contract_cols(
            trio[at, 2 * ff :], up_w[...]
        )


def early(x):
    return pl.pallas_call(
        lambda x_ref, out_ref: None,
        out_shape=jax.ShapeDtypeStruct(x.shape, x.dtype),
        in_specs=[pl.BlockSpec(memory_space=pltpu.HBM)],
        out_specs=pl.BlockSpec(memory_space=pltpu.HBM),
        input_output_aliases={0: 0},
        cost_estimate=pl.CostEstimate(flops=10**11, bytes_accessed=0, transcendentals=0),
        name="exchanged",
    )(x)


def turn(x, size, step):
    return lax.ppermute(x, ("zh", "zl"), [(i, (i + step) % size) for i in range(size)])


def pick(first, x):
    return jnp.where(first, x[:, 0], x[:, 1])


def per_device(zh_size, blocks, tokens, out_grad, gate_weight, up_weight, down_weight):
    zl = lax.axis_index("zl")
    xh = lax.axis_index("xh")
    first = zl == 0
    rows, depth = tokens.shape
    ff = gate_weight.shape[1]
    group = 2 * zh_size

    far = swap(jnp.concatenate([gate_weight, up_weight, down_weight], axis=0), "zl")

    shard = jnp.concatenate([tokens, out_grad], axis=1)
    own = lax.all_to_all(
        jnp.broadcast_to(shard[None], (blocks, rows, 2 * depth)), ("y", "xl"), 0, 0, tiled=True
    )
    own, far = lax.optimization_barrier((own, early(far)))
    own = own.reshape(zh_size // 2, 2, -1, 2 * depth)
    ext = swap(pick(~first, own), "zl").reshape(-1, 2 * depth)
    other = swap(own, "c")
    ext_other = swap(ext, "c")

    half_tokens = own.size // (2 * depth)
    token_rows = half_tokens // group
    sent_rows = 3 * (ff // LANES) * token_rows
    parts = pl.pallas_call(
        forward_kernel,
        out_shape=jax.ShapeDtypeStruct((group, sent_rows + TAIL, LANES), jnp.float32),
        in_specs=[pl.BlockSpec(memory_space=pltpu.SMEM)]
        + [pl.BlockSpec(memory_space=pltpu.VMEM)] * 8,
        out_specs=pl.BlockSpec(memory_space=pltpu.VMEM),
        compiler_params=pltpu.CompilerParams(vmem_limit_bytes=40 * 2**20),
        cost_estimate=pl.CostEstimate(
            flops=12 * half_tokens * depth * ff,
            bytes_accessed=9 * 2**20,
            transcendentals=0,
        ),
        name="forward_sums",
    )(
        zl.astype(jnp.int32)[None], own, other, ext, ext_other,
        gate_weight, up_weight, down_weight, far,
    )
    parts = lax.all_to_all(parts.astype(jnp.float16), ("zh", "xh"), 0, 0, tiled=True)
    trio = pl.pallas_call(
        middle_kernel,
        out_shape=jax.ShapeDtypeStruct((token_rows, 3 * ff), jnp.bfloat16),
        in_specs=[pl.BlockSpec(memory_space=pltpu.VMEM)],
        out_specs=pl.BlockSpec(memory_space=pltpu.VMEM),
        compiler_params=pltpu.CompilerParams(vmem_limit_bytes=24 * 2**20),
        cost_estimate=pl.CostEstimate(
            flops=8 * group * token_rows * ff,
            bytes_accessed=4 * 2**20,
            transcendentals=token_rows * ff,
        ),
        name="hidden_and_grads",
    )(parts.astype(jnp.float32))

    right, left = [trio], [trio]
    beside = [swap(trio, "xh")]
    for step in range(1, zh_size):
        right.append(turn(right[-1], 2 * zh_size, 1))
        left.append(turn(left[-1], 2 * zh_size, -1))
        if step >= 2:
            right[-1], left[-1], beside[step - 2] = lax.optimization_barrier(
                (right[-1], left[-1], beside[step - 2])
            )
        beside.append(swap(jnp.concatenate([right[-1], left[-1]], axis=0), "xh"))
    right.append(turn(right[-1], 2 * zh_size, 1))
    beside.append(swap(right[-1], "xh"))

    place = jnp.stack([2 * lax.axis_index("zh") + zl, xh]).astype(jnp.int32)
    blocks_in = [trio] + right[1:] + left[1:] + beside
    share = half_tokens
    trio, in_own, in_other = pl.pallas_call(
        functools.partial(backward_kernel, zh_size),
        out_shape=(
            jax.ShapeDtypeStruct((2 * share, 3 * ff), jnp.bfloat16),
            jax.ShapeDtypeStruct((share, depth), jnp.float32),
            jax.ShapeDtypeStruct((share, depth), jnp.float32),
        ),
        in_specs=[pl.BlockSpec(memory_space=pltpu.SMEM)]
        + [pl.BlockSpec(memory_space=pltpu.VMEM)] * (2 + len(blocks_in)),
        out_specs=[pl.BlockSpec(memory_space=pltpu.VMEM)] * 3,
        compiler_params=pltpu.CompilerParams(vmem_limit_bytes=40 * 2**20),
        cost_estimate=pl.CostEstimate(
            flops=8 * share * depth * ff, bytes_accessed=9 * 2**20, transcendentals=0
        ),
        name="input_gradient",
    )(place, gate_weight, up_weight, *blocks_in)
    hidden, gate_grad, up_grad = trio[:, :ff], trio[:, ff : 2 * ff], trio[:, 2 * ff :]

    every = jnp.concatenate([x.reshape(-1, 2 * depth) for x in (own, other)], axis=0)
    inputs, grads = every[:, :depth], every[:, depth:]
    in_part = in_own + swap(in_other, "c")
    in_part = lax.all_to_all(
        in_part.astype(jnp.bfloat16).reshape(blocks, rows, depth), ("y", "xl"), 0, 0, tiled=True
    )
    in_grad = jnp.sum(in_part.astype(jnp.float32), axis=0).astype(jnp.bfloat16)

    down_wgrad = contract_rows(hidden, grads).astype(jnp.bfloat16)
    gate_wgrad = contract_rows(inputs, gate_grad).astype(jnp.bfloat16)
    up_wgrad = contract_rows(inputs, up_grad).astype(jnp.bfloat16)
    return (in_grad, gate_wgrad, up_wgrad, down_wgrad)


def solution(mesh):
    row, col = mesh.devices.shape
    zh_size, y_size = row // 4, col // 4
    fine = Mesh(
        mesh.devices.reshape(zh_size, 2, 2, y_size, 2, 2), ("zh", "zl", "xh", "y", "xl", "c")
    )

    def body(*args):
        return per_device(zh_size, 2 * y_size, *args)

    in_specs = (P(COL, ROW), P(COL, ROW), P(ROW, COL), P(ROW, COL), P(COL, ROW))
    out_specs = (P(COL, ROW), P(ROW, COL), P(ROW, COL), P(COL, ROW))
    return jax.shard_map(
        body, mesh=fine, in_specs=in_specs, out_specs=out_specs, check_vma=False
    )
```

```python
import functools

import jax
import jax.numpy as jnp
from jax import lax
from jax.experimental import pallas as pl
from jax.experimental.pallas import tpu as pltpu
from jax.sharding import Mesh, PartitionSpec as P

ROW = ("zh", "zl", "xh")
COL = ("y", "xl", "c")
LANES = 128
TAIL = 16


def swiglu_back(gate, up, hidden_grad):
    sig = jax.nn.sigmoid(gate)
    act = gate * sig
    hidden = (act * up).astype(jnp.bfloat16)
    gate_grad = (hidden_grad * up * sig * (1.0 + gate * (1.0 - sig))).astype(jnp.bfloat16)
    up_grad = (hidden_grad * act).astype(jnp.bfloat16)
    return (hidden, gate_grad, up_grad)


def contract_rows(left, right):
    return lax.dot_general(
        left, right, (((0,), (0,)), ((), ())), preferred_element_type=jnp.float32
    )


def contract_cols(left, right):
    return lax.dot_general(
        left, right, (((1,), (1,)), ((), ())), preferred_element_type=jnp.float32
    )


def matmul(left, right):
    return jnp.dot(left, right, preferred_element_type=jnp.float32)


def swap(x, axis):
    return lax.ppermute(x, axis, [(0, 1), (1, 0)])


def forward_kernel(half_ref, own, other, ext, ext_other, gate_w, up_w, down_w, far, out):
    half = half_ref[0]
    depth = gate_w.shape[0]
    near = [source[i, half] for source in (own, other) for i in range(own.shape[0])]
    near = jnp.concatenate(near, axis=0)
    beyond = jnp.concatenate([ext[...], ext_other[...]], axis=0)
    group, rows = out.shape[0], near.shape[0] // out.shape[0]
    lane_blocks = gate_w.shape[1] // LANES
    place = lax.broadcasted_iota(jnp.int32, (TAIL, LANES), 0)
    tail = jnp.zeros((TAIL, LANES), jnp.float32)
    for n in range(3):
        far_w = far[n * depth : (n + 1) * depth, :]
        if n == 2:
            part = contract_cols(near[:, depth:], down_w[...]) + contract_cols(
                beyond[:, depth:], far_w
            )
        else:
            near_w = (gate_w, up_w)[n][...]
            part = matmul(near[:, :depth], near_w) + matmul(beyond[:, :depth], far_w)
        top = jnp.max(jnp.abs(part), axis=0, keepdims=True)
        top = jnp.max(top, axis=1, keepdims=True)
        exponent = jnp.floor(14.0 - jnp.log2(jnp.maximum(top, 1e-30)))
        exponent = jnp.clip(exponent, -100.0, 100.0)
        part = part * jnp.exp2(exponent)
        for j in range(group):
            for q in range(lane_blocks):
                at = (n * lane_blocks + q) * rows
                out[j, at : at + rows, :] = part[
                    j * rows : (j + 1) * rows, q * LANES : (q + 1) * LANES
                ]
        tail = jnp.where(place == n, exponent, tail)
    for j in range(group):
        out[j, 3 * lane_blocks * rows :, :] = tail


def middle_kernel(parts, trio):
    rows, ff = trio.shape[0], trio.shape[1] // 3
    lane_blocks = ff // LANES
    tail = 3 * lane_blocks * rows
    scales = [jnp.exp2(-parts[:, tail + n : tail + n + 1, :]) for n in range(3)]
    for q in range(lane_blocks):
        sums = []
        for n in range(3):
            at = (n * lane_blocks + q) * rows
            sums.append(jnp.sum(parts[:, at : at + rows, :] * scales[n], axis=0))
        for n, value in enumerate(swiglu_back(*sums)):
            at = n * ff + q * LANES
            trio[:, at : at + LANES] = value


def backward_kernel(zh_size, gate_w, up_w, trio_in, *refs):
    size = 2 * zh_size
    rights, refs = refs[:zh_size], refs[zh_size:]
    lefts, refs = refs[: zh_size - 1], refs[zh_size - 1 :]
    beside, (trio_out, in_own, in_other, trio, arrived, left) = refs[:zh_size], refs[zh_size:]
    rows, ff = trio_in.shape[0], gate_w.shape[1]
    z, xh = 2 * lax.axis_index("zh") + lax.axis_index("zl"), lax.axis_index("xh")
    copies = []

    def put(distance, mine, others):
        block = 2 * rows * lax.rem(z + distance + size, size)
        for source, half in ((mine, xh), (others, 1 - xh)):
            at = pl.multiple_of(block + rows * half, rows)
            copies.append(
                pltpu.make_async_copy(
                    source, trio.at[pl.ds(at, rows), :], arrived.at[len(copies)]
                )
            )
            copies[-1].start()

    put(0, trio_in, beside[0].at[pl.ds(0, rows), :])
    for k in range(1, zh_size):
        others = beside[k - 1]
        at = others.shape[0] - 2 * rows
        put(-k, rights[k - 1], others.at[pl.ds(at, rows), :])
        put(k, lefts[k - 1], others.at[pl.ds(at + rows, rows), :])
    put(-zh_size, rights[-1], beside[-1])
    for copy in copies:
        copy.wait()
    copy = pltpu.make_async_copy(trio, trio_out, left)
    copy.start()
    share = in_own.shape[0]
    for part, target in ((1, in_other), (0, in_own)):
        at = slice(part * share, (part + 1) * share)
        target[...] = contract_cols(trio[at, ff : 2 * ff], gate_w[...]) + contract_cols(
            trio[at, 2 * ff :], up_w[...]
        )
    copy.wait()


def pair_swap(x, zh_size):
    size = 2 * zh_size
    pairs = [
        (2 * z + c, 2 * ((z + (1 if z % 2 == c else -1)) % size) + c)
        for z in range(size)
        for c in range(2)
    ]
    return lax.ppermute(x, ("zh", "zl", "c"), pairs)


def turn(x, size, step):
    return lax.ppermute(x, ("zh", "zl"), [(i, (i + step) % size) for i in range(size)])


def pick(first, x):
    return jnp.where(first, x[:, 0], x[:, 1])


def per_device(zh_size, blocks, tokens, out_grad, gate_weight, up_weight, down_weight):
    zl = lax.axis_index("zl")
    xh = lax.axis_index("xh")
    first = zl == 0
    rows, depth = tokens.shape
    ff = gate_weight.shape[1]
    group = 2 * zh_size

    far = pair_swap(jnp.concatenate([gate_weight, up_weight, down_weight], axis=0), zh_size)

    shard = jnp.concatenate([tokens, out_grad], axis=1)
    own = lax.all_to_all(
        jnp.broadcast_to(shard[None], (blocks, rows, 2 * depth)), ("y", "xl"), 0, 0, tiled=True
    )
    own, far = lax.optimization_barrier((own, far))
    own = own.reshape(zh_size // 2, 2, -1, 2 * depth)
    other = swap(own, "c")
    ext = pair_swap(pick(~first, own), zh_size).reshape(-1, 2 * depth)
    ext_other = pair_swap(pick(~first, other), zh_size).reshape(-1, 2 * depth)

    half_tokens = own.size // (2 * depth)
    token_rows = half_tokens // group
    sent_rows = 3 * (ff // LANES) * token_rows
    parts = pl.pallas_call(
        forward_kernel,
        out_shape=jax.ShapeDtypeStruct((group, sent_rows + TAIL, LANES), jnp.float32),
        in_specs=[pl.BlockSpec(memory_space=pltpu.SMEM)]
        + [pl.BlockSpec(memory_space=pltpu.VMEM)] * 8,
        out_specs=pl.BlockSpec(memory_space=pltpu.VMEM),
        compiler_params=pltpu.CompilerParams(vmem_limit_bytes=40 * 2**20),
        cost_estimate=pl.CostEstimate(
            flops=12 * half_tokens * depth * ff,
            bytes_accessed=9 * 2**20,
            transcendentals=0,
        ),
        name="forward_sums",
    )(
        zl.astype(jnp.int32)[None], own, other, ext, ext_other,
        gate_weight, up_weight, down_weight, far,
    )
    parts = lax.all_to_all(parts.astype(jnp.float16), ("zh", "xh"), 0, 0, tiled=True)
    trio = pl.pallas_call(
        middle_kernel,
        out_shape=jax.ShapeDtypeStruct((token_rows, 3 * ff), jnp.bfloat16),
        in_specs=[pl.BlockSpec(memory_space=pltpu.VMEM)],
        out_specs=pl.BlockSpec(memory_space=pltpu.VMEM),
        compiler_params=pltpu.CompilerParams(vmem_limit_bytes=24 * 2**20),
        cost_estimate=pl.CostEstimate(
            flops=8 * group * token_rows * ff,
            bytes_accessed=4 * 2**20,
            transcendentals=token_rows * ff,
        ),
        name="hidden_and_grads",
    )(parts.astype(jnp.float32))

    right, left, beside = [trio], [trio], []
    waiting = [trio]
    for step in range(1, zh_size):
        right.append(turn(right[-1], 2 * zh_size, 1))
        left.append(turn(left[-1], 2 * zh_size, -1))
        waiting = waiting + [right[-1], left[-1]]
        if step >= 3:
            right[-1], left[-1], beside[step - 3] = lax.optimization_barrier(
                (right[-1], left[-1], beside[step - 3])
            )
            waiting = [right[-1], left[-1]]
        beside.append(swap(jnp.concatenate(waiting, axis=0), "xh"))
        waiting = []
    right.append(turn(right[-1], 2 * zh_size, 1))
    beside.append(swap(right[-1], "xh"))

    blocks_in = [trio] + right[1:] + left[1:] + beside
    share = half_tokens
    trio, in_own, in_other = pl.pallas_call(
        functools.partial(backward_kernel, zh_size),
        out_shape=(
            jax.ShapeDtypeStruct((2 * share, 3 * ff), jnp.bfloat16),
            jax.ShapeDtypeStruct((share, depth), jnp.float32),
            jax.ShapeDtypeStruct((share, depth), jnp.float32),
        ),
        in_specs=[pl.BlockSpec(memory_space=pltpu.VMEM)] * 2
        + [pl.BlockSpec(memory_space=pltpu.HBM)] * len(blocks_in),
        out_specs=[pl.BlockSpec(memory_space=pltpu.HBM)]
        + [pl.BlockSpec(memory_space=pltpu.VMEM)] * 2,
        scratch_shapes=[
            pltpu.VMEM((2 * share, 3 * ff), jnp.bfloat16),
            pltpu.SemaphoreType.DMA((4 * zh_size,)),
            pltpu.SemaphoreType.DMA,
        ],
        compiler_params=pltpu.CompilerParams(vmem_limit_bytes=40 * 2**20),
        cost_estimate=pl.CostEstimate(
            flops=8 * share * depth * ff, bytes_accessed=9 * 2**20, transcendentals=0
        ),
        name="input_gradient",
    )(gate_weight, up_weight, *blocks_in)
    hidden, gate_grad, up_grad = trio[:, :ff], trio[:, ff : 2 * ff], trio[:, 2 * ff :]

    every = jnp.concatenate([x.reshape(-1, 2 * depth) for x in (own, other)], axis=0)
    inputs, grads = every[:, :depth], every[:, depth:]
    in_part = in_own + swap(in_other, "c")
    in_part = lax.all_to_all(
        in_part.astype(jnp.bfloat16).reshape(blocks, rows, depth), ("y", "xl"), 0, 0, tiled=True
    )
    in_grad = jnp.sum(in_part.astype(jnp.float32), axis=0).astype(jnp.bfloat16)

    down_wgrad = contract_rows(hidden, grads).astype(jnp.bfloat16)
    gate_wgrad = contract_rows(inputs, gate_grad).astype(jnp.bfloat16)
    up_wgrad = contract_rows(inputs, up_grad).astype(jnp.bfloat16)
    return (in_grad, gate_wgrad, up_wgrad, down_wgrad)


def solution(mesh):
    row, col = mesh.devices.shape
    zh_size, y_size = row // 4, col // 4
    fine = Mesh(
        mesh.devices.reshape(zh_size, 2, 2, y_size, 2, 2), ("zh", "zl", "xh", "y", "xl", "c")
    )

    def body(*args):
        return per_device(zh_size, 2 * y_size, *args)

    in_specs = (P(COL, ROW), P(COL, ROW), P(ROW, COL), P(ROW, COL), P(COL, ROW))
    out_specs = (P(COL, ROW), P(ROW, COL), P(ROW, COL), P(COL, ROW))
    return jax.shard_map(
        body, mesh=fine, in_specs=in_specs, out_specs=out_specs, check_vma=False
    )
```

```python
import functools

import jax
import jax.numpy as jnp
from jax import lax
from jax.experimental import pallas as pl
from jax.experimental.pallas import tpu as pltpu
from jax.sharding import Mesh, PartitionSpec as P

ROW = ("zh", "zl", "xh")
COL = ("y", "xl", "c")
LANES = 128
TAIL = 16


def swiglu_back(gate, up, hidden_grad):
    sig = jax.nn.sigmoid(gate)
    act = gate * sig
    hidden = (act * up).astype(jnp.bfloat16)
    gate_grad = (hidden_grad * up * sig * (1.0 + gate * (1.0 - sig))).astype(jnp.bfloat16)
    up_grad = (hidden_grad * act).astype(jnp.bfloat16)
    return (hidden, gate_grad, up_grad)


def contract_rows(left, right):
    return lax.dot_general(
        left, right, (((0,), (0,)), ((), ())), preferred_element_type=jnp.float32
    )


def contract_cols(left, right):
    return lax.dot_general(
        left, right, (((1,), (1,)), ((), ())), preferred_element_type=jnp.float32
    )


def matmul(left, right):
    return jnp.dot(left, right, preferred_element_type=jnp.float32)


def swap(x, axis):
    return lax.ppermute(x, axis, [(0, 1), (1, 0)])


def forward_kernel(half_ref, own, other, ext, ext_other, gate_w, up_w, down_w, far, out):
    half = half_ref[0]
    depth = gate_w.shape[0]
    near = [source[i, half] for source in (own, other) for i in range(own.shape[0])]
    near = jnp.concatenate(near, axis=0)
    beyond = jnp.concatenate([ext[...], ext_other[...]], axis=0)
    group, rows = out.shape[0], near.shape[0] // out.shape[0]
    lane_blocks = gate_w.shape[1] // LANES
    place = lax.broadcasted_iota(jnp.int32, (TAIL, LANES), 0)
    tail = jnp.zeros((TAIL, LANES), jnp.float32)
    for n in range(3):
        far_w = far[n * depth : (n + 1) * depth, :]
        if n == 2:
            part = contract_cols(near[:, depth:], down_w[...]) + contract_cols(
                beyond[:, depth:], far_w
            )
        else:
            near_w = (gate_w, up_w)[n][...]
            part = matmul(near[:, :depth], near_w) + matmul(beyond[:, :depth], far_w)
        top = jnp.max(jnp.abs(part), axis=0, keepdims=True)
        top = jnp.max(top, axis=1, keepdims=True)
        exponent = jnp.floor(14.0 - jnp.log2(jnp.maximum(top, 1e-30)))
        exponent = jnp.clip(exponent, -100.0, 100.0)
        part = part * jnp.exp2(exponent)
        for j in range(group):
            for q in range(lane_blocks):
                at = (n * lane_blocks + q) * rows
                out[j, at : at + rows, :] = part[
                    j * rows : (j + 1) * rows, q * LANES : (q + 1) * LANES
                ]
        tail = jnp.where(place == n, exponent, tail)
    for j in range(group):
        out[j, 3 * lane_blocks * rows :, :] = tail


def middle_kernel(parts, trio):
    rows, ff = trio.shape[0], trio.shape[1] // 3
    lane_blocks = ff // LANES
    tail = 3 * lane_blocks * rows
    scales = [jnp.exp2(-parts[:, tail + n : tail + n + 1, :]) for n in range(3)]
    for q in range(lane_blocks):
        sums = []
        for n in range(3):
            at = (n * lane_blocks + q) * rows
            sums.append(jnp.sum(parts[:, at : at + rows, :] * scales[n], axis=0))
        for n, value in enumerate(swiglu_back(*sums)):
            at = n * ff + q * LANES
            trio[:, at : at + LANES] = value


def order_blocks(zh_size, refs, trio, arrived, skip=0):
    size = 2 * zh_size
    trio_in, rights, refs = refs[0], refs[1 : 1 + zh_size], refs[1 + zh_size :]
    lefts, beside = refs[: zh_size - 1], refs[zh_size - 1 :]
    rows = trio_in.shape[0]
    z, xh = 2 * lax.axis_index("zh") + lax.axis_index("zl"), lax.axis_index("xh")
    copies = []

    def put(distance, mine, others):
        block = 2 * rows * lax.rem(z + distance + size, size)
        for source, half in ((mine, xh), (others, 1 - xh)):
            if skip:
                source = source.at[:, pl.ds(skip, source.shape[1] - skip)]
            at = pl.multiple_of(block + rows * half, rows)
            copies.append(
                pltpu.make_async_copy(
                    source, trio.at[pl.ds(at, rows), :], arrived.at[len(copies)]
                )
            )
            copies[-1].start()

    put(0, trio_in, beside[0].at[pl.ds(0, rows), :])
    for k in range(1, zh_size):
        others = beside[k - 1]
        at = others.shape[0] - 2 * rows
        put(-k, rights[k - 1], others.at[pl.ds(at, rows), :])
        put(k, lefts[k - 1], others.at[pl.ds(at + rows, rows), :])
    put(-zh_size, rights[-1], beside[-1])
    for copy in copies:
        copy.wait()


def input_kernel(zh_size, gate_w, up_w, *refs):
    blocks_in, (in_own, in_other, duo, arrived) = refs[:-4], refs[-4:]
    share, ff = in_own.shape[0], gate_w.shape[1]
    order_blocks(zh_size, blocks_in, duo, arrived, ff)
    for part, target in ((1, in_other), (0, in_own)):
        at = slice(part * share, (part + 1) * share)
        target[...] = contract_cols(duo[at, :ff], gate_w[...]) + contract_cols(
            duo[at, ff:], up_w[...]
        )


def weight_kernel(zh_size, own, other, *refs):
    blocks_in, (gate_wgrad, up_wgrad, down_wgrad, trio, arrived) = refs[:-5], refs[-5:]
    order_blocks(zh_size, blocks_in, trio, arrived)
    depth, ff = gate_wgrad.shape
    every = [x[...].reshape(-1, 2 * depth) for x in (own, other)]
    every = jnp.concatenate(every, axis=0)
    inputs, grads = every[:, :depth], every[:, depth:]
    down_wgrad[...] = contract_rows(trio[:, :ff], grads).astype(jnp.bfloat16)
    gate_wgrad[...] = contract_rows(inputs, trio[:, ff : 2 * ff]).astype(jnp.bfloat16)
    up_wgrad[...] = contract_rows(inputs, trio[:, 2 * ff :]).astype(jnp.bfloat16)


def pair_swap(x, zh_size):
    size = 2 * zh_size
    pairs = [
        (2 * z + c, 2 * ((z + (1 if z % 2 == c else -1)) % size) + c)
        for z in range(size)
        for c in range(2)
    ]
    return lax.ppermute(x, ("zh", "zl", "c"), pairs)


def turn(x, size, step):
    return lax.ppermute(x, ("zh", "zl"), [(i, (i + step) % size) for i in range(size)])


def pick(first, x):
    return jnp.where(first, x[:, 0], x[:, 1])


def per_device(zh_size, blocks, tokens, out_grad, gate_weight, up_weight, down_weight):
    zl = lax.axis_index("zl")
    xh = lax.axis_index("xh")
    first = zl == 0
    rows, depth = tokens.shape
    ff = gate_weight.shape[1]
    group = 2 * zh_size

    far = pair_swap(jnp.concatenate([gate_weight, up_weight, down_weight], axis=0), zh_size)

    shard = jnp.concatenate([tokens, out_grad], axis=1)
    own = lax.all_to_all(
        jnp.broadcast_to(shard[None], (blocks, rows, 2 * depth)), ("y", "xl"), 0, 0, tiled=True
    )
    own, far = lax.optimization_barrier((own, far))
    own = own.reshape(zh_size // 2, 2, -1, 2 * depth)
    other = swap(own, "c")
    ext = pair_swap(pick(~first, own), zh_size).reshape(-1, 2 * depth)
    ext_other = pair_swap(pick(~first, other), zh_size).reshape(-1, 2 * depth)

    half_tokens = own.size // (2 * depth)
    token_rows = half_tokens // group
    sent_rows = 3 * (ff // LANES) * token_rows
    parts = pl.pallas_call(
        forward_kernel,
        out_shape=jax.ShapeDtypeStruct((group, sent_rows + TAIL, LANES), jnp.float32),
        in_specs=[pl.BlockSpec(memory_space=pltpu.SMEM)]
        + [pl.BlockSpec(memory_space=pltpu.VMEM)] * 8,
        out_specs=pl.BlockSpec(memory_space=pltpu.VMEM),
        compiler_params=pltpu.CompilerParams(vmem_limit_bytes=40 * 2**20),
        cost_estimate=pl.CostEstimate(
            flops=12 * half_tokens * depth * ff,
            bytes_accessed=9 * 2**20,
            transcendentals=0,
        ),
        name="forward_sums",
    )(
        zl.astype(jnp.int32)[None], own, other, ext, ext_other,
        gate_weight, up_weight, down_weight, far,
    )
    parts = lax.all_to_all(parts.astype(jnp.float16), ("zh", "xh"), 0, 0, tiled=True)
    trio = pl.pallas_call(
        middle_kernel,
        out_shape=jax.ShapeDtypeStruct((token_rows, 3 * ff), jnp.bfloat16),
        in_specs=[pl.BlockSpec(memory_space=pltpu.VMEM)],
        out_specs=pl.BlockSpec(memory_space=pltpu.VMEM),
        compiler_params=pltpu.CompilerParams(vmem_limit_bytes=24 * 2**20),
        cost_estimate=pl.CostEstimate(
            flops=8 * group * token_rows * ff,
            bytes_accessed=4 * 2**20,
            transcendentals=token_rows * ff,
        ),
        name="hidden_and_grads",
    )(parts.astype(jnp.float32))

    right, left, beside = [trio], [trio], []
    waiting = [trio]
    for step in range(1, zh_size):
        right.append(turn(right[-1], 2 * zh_size, 1))
        left.append(turn(left[-1], 2 * zh_size, -1))
        waiting = waiting + [right[-1], left[-1]]
        if step >= 3:
            right[-1], left[-1], beside[step - 3] = lax.optimization_barrier(
                (right[-1], left[-1], beside[step - 3])
            )
            waiting = [right[-1], left[-1]]
        beside.append(swap(jnp.concatenate(waiting, axis=0), "xh"))
        waiting = []
    right.append(turn(right[-1], 2 * zh_size, 1))
    beside.append(swap(right[-1], "xh"))

    blocks_in = [trio] + right[1:] + left[1:] + beside
    share = half_tokens
    vmem, hbm = pl.BlockSpec(memory_space=pltpu.VMEM), pl.BlockSpec(memory_space=pltpu.HBM)

    def ordering(width):
        return [
            pltpu.VMEM((2 * share, width), jnp.bfloat16),
            pltpu.SemaphoreType.DMA((4 * zh_size,)),
        ]

    in_own, in_other = pl.pallas_call(
        functools.partial(input_kernel, zh_size),
        out_shape=[jax.ShapeDtypeStruct((share, depth), jnp.float32)] * 2,
        in_specs=[vmem] * 2 + [hbm] * len(blocks_in),
        out_specs=[vmem] * 2,
        scratch_shapes=ordering(2 * ff),
        compiler_params=pltpu.CompilerParams(vmem_limit_bytes=40 * 2**20),
        cost_estimate=pl.CostEstimate(
            flops=8 * share * depth * ff, bytes_accessed=9 * 2**20, transcendentals=0
        ),
        name="input_gradient",
    )(gate_weight, up_weight, *blocks_in)
    in_part = in_own + swap(in_other, "c")
    in_part = lax.all_to_all(
        in_part.astype(jnp.bfloat16).reshape(blocks, rows, depth), ("y", "xl"), 0, 0, tiled=True
    )
    in_grad = jnp.sum(in_part.astype(jnp.float32), axis=0).astype(jnp.bfloat16)

    gate_wgrad, up_wgrad, down_wgrad = pl.pallas_call(
        functools.partial(weight_kernel, zh_size),
        out_shape=[
            jax.ShapeDtypeStruct((depth, ff), jnp.bfloat16),
            jax.ShapeDtypeStruct((depth, ff), jnp.bfloat16),
            jax.ShapeDtypeStruct((ff, depth), jnp.bfloat16),
        ],
        in_specs=[vmem] * 2 + [hbm] * len(blocks_in),
        out_specs=[vmem] * 3,
        scratch_shapes=ordering(3 * ff),
        compiler_params=pltpu.CompilerParams(vmem_limit_bytes=40 * 2**20),
        cost_estimate=pl.CostEstimate(
            flops=12 * share * depth * ff, bytes_accessed=9 * 2**20, transcendentals=0
        ),
        name="weight_gradients",
    )(own, other, *blocks_in)
    return (in_grad, gate_wgrad, up_wgrad, down_wgrad)


def solution(mesh):
    row, col = mesh.devices.shape
    zh_size, y_size = row // 4, col // 4
    fine = Mesh(
        mesh.devices.reshape(zh_size, 2, 2, y_size, 2, 2), ("zh", "zl", "xh", "y", "xl", "c")
    )

    def body(*args):
        return per_device(zh_size, 2 * y_size, *args)

    in_specs = (P(COL, ROW), P(COL, ROW), P(ROW, COL), P(ROW, COL), P(COL, ROW))
    out_specs = (P(COL, ROW), P(ROW, COL), P(ROW, COL), P(COL, ROW))
    return jax.shard_map(
        body, mesh=fine, in_specs=in_specs, out_specs=out_specs, check_vma=False
    )
```

```python
import functools

import jax
import jax.numpy as jnp
from jax import lax
from jax.experimental import pallas as pl
from jax.experimental.pallas import tpu as pltpu
from jax.sharding import Mesh, PartitionSpec as P

ROW = ("zh", "zl", "xh")
COL = ("y", "xl", "c")
LANES = 128
TAIL = 16


def swiglu_back(gate, up, hidden_grad):
    sig = jax.nn.sigmoid(gate)
    act = gate * sig
    hidden = (act * up).astype(jnp.bfloat16)
    gate_grad = (hidden_grad * up * sig * (1.0 + gate * (1.0 - sig))).astype(jnp.bfloat16)
    up_grad = (hidden_grad * act).astype(jnp.bfloat16)
    return (hidden, gate_grad, up_grad)


def contract_rows(left, right):
    return lax.dot_general(
        left, right, (((0,), (0,)), ((), ())), preferred_element_type=jnp.float32
    )


def contract_cols(left, right):
    return lax.dot_general(
        left, right, (((1,), (1,)), ((), ())), preferred_element_type=jnp.float32
    )


def matmul(left, right):
    return jnp.dot(left, right, preferred_element_type=jnp.float32)


def swap(x, axis):
    return lax.ppermute(x, axis, [(0, 1), (1, 0)])


def forward_kernel(half_ref, own, other, ext, ext_other, gate_w, up_w, down_w, far, out):
    half = half_ref[0]
    depth = gate_w.shape[0]
    near = [source[i, half] for source in (own, other) for i in range(own.shape[0])]
    near = jnp.concatenate(near, axis=0)
    beyond = jnp.concatenate([ext[...], ext_other[...]], axis=0)
    group, rows = out.shape[0], near.shape[0] // out.shape[0]
    lane_blocks = gate_w.shape[1] // LANES
    place = lax.broadcasted_iota(jnp.int32, (TAIL, LANES), 0)
    tail = jnp.zeros((TAIL, LANES), jnp.float32)
    for n in range(3):
        far_w = far[n * depth : (n + 1) * depth, :]
        if n == 2:
            part = contract_cols(near[:, depth:], down_w[...]) + contract_cols(
                beyond[:, depth:], far_w
            )
        else:
            near_w = (gate_w, up_w)[n][...]
            part = matmul(near[:, :depth], near_w) + matmul(beyond[:, :depth], far_w)
        top = jnp.max(jnp.abs(part), axis=0, keepdims=True)
        top = jnp.max(top, axis=1, keepdims=True)
        exponent = jnp.floor(14.0 - jnp.log2(jnp.maximum(top, 1e-30)))
        exponent = jnp.clip(exponent, -100.0, 100.0)
        part = part * jnp.exp2(exponent)
        for j in range(group):
            for q in range(lane_blocks):
                at = (n * lane_blocks + q) * rows
                out[j, at : at + rows, :] = part[
                    j * rows : (j + 1) * rows, q * LANES : (q + 1) * LANES
                ]
        tail = jnp.where(place == n, exponent, tail)
    for j in range(group):
        out[j, 3 * lane_blocks * rows :, :] = tail


def middle_kernel(parts, trio):
    rows, ff = trio.shape[0], trio.shape[1] // 3
    lane_blocks = ff // LANES
    tail = 3 * lane_blocks * rows
    scales = [jnp.exp2(-parts[:, tail + n : tail + n + 1, :]) for n in range(3)]
    for q in range(lane_blocks):
        sums = []
        for n in range(3):
            at = (n * lane_blocks + q) * rows
            sums.append(jnp.sum(parts[:, at : at + rows, :] * scales[n], axis=0))
        for n, value in enumerate(swiglu_back(*sums)):
            at = n * ff + q * LANES
            trio[:, at : at + LANES] = value


def order_blocks(zh_size, refs, trio, arrived, skip=0):
    size = 2 * zh_size
    trio_in, rights, refs = refs[0], refs[1 : 1 + zh_size], refs[1 + zh_size :]
    lefts, beside = refs[: zh_size - 1], refs[zh_size - 1 :]
    rows = trio_in.shape[0]
    z, xh = 2 * lax.axis_index("zh") + lax.axis_index("zl"), lax.axis_index("xh")
    copies = []

    def put(distance, mine, others):
        block = 2 * rows * lax.rem(z + distance + size, size)
        for source, half in ((mine, xh), (others, 1 - xh)):
            if skip:
                source = source.at[:, pl.ds(skip, source.shape[1] - skip)]
            at = pl.multiple_of(block + rows * half, rows)
            copies.append(
                pltpu.make_async_copy(
                    source, trio.at[pl.ds(at, rows), :], arrived.at[len(copies)]
                )
            )
            copies[-1].start()

    put(0, trio_in, beside[0].at[pl.ds(0, rows), :])
    for k in range(1, zh_size):
        others = beside[k - 1]
        at = others.shape[0] - 2 * rows
        put(-k, rights[k - 1], others.at[pl.ds(at, rows), :])
        put(k, lefts[k - 1], others.at[pl.ds(at + rows, rows), :])
    put(-zh_size, rights[-1], beside[-1])
    for copy in copies:
        copy.wait()


def input_kernel(zh_size, gate_w, up_w, *refs):
    blocks_in, (in_own, in_other, duo, arrived) = refs[:-4], refs[-4:]
    share, ff = in_own.shape[0], gate_w.shape[1]
    order_blocks(zh_size, blocks_in, duo, arrived, ff)
    for part, target in ((1, in_other), (0, in_own)):
        at = slice(part * share, (part + 1) * share)
        total = contract_cols(duo[at, :ff], gate_w[...]) + contract_cols(duo[at, ff:], up_w[...])
        target[...] = total.astype(target.dtype)


def weight_kernel(zh_size, own, other, *refs):
    blocks_in, (gate_wgrad, up_wgrad, down_wgrad, trio, arrived) = refs[:-5], refs[-5:]
    order_blocks(zh_size, blocks_in, trio, arrived)
    depth, ff = gate_wgrad.shape
    every = [x[...].reshape(-1, 2 * depth) for x in (own, other)]
    every = jnp.concatenate(every, axis=0)
    inputs, grads = every[:, :depth], every[:, depth:]
    down_wgrad[...] = contract_rows(trio[:, :ff], grads).astype(jnp.bfloat16)
    gate_wgrad[...] = contract_rows(inputs, trio[:, ff : 2 * ff]).astype(jnp.bfloat16)
    up_wgrad[...] = contract_rows(inputs, trio[:, 2 * ff :]).astype(jnp.bfloat16)


def pair_swap(x, zh_size):
    size = 2 * zh_size
    pairs = [
        (2 * z + c, 2 * ((z + (1 if z % 2 == c else -1)) % size) + c)
        for z in range(size)
        for c in range(2)
    ]
    return lax.ppermute(x, ("zh", "zl", "c"), pairs)


def turn(x, size, step):
    return lax.ppermute(x, ("zh", "zl"), [(i, (i + step) % size) for i in range(size)])


def pick(first, x):
    return jnp.where(first, x[:, 0], x[:, 1])


def per_device(zh_size, blocks, tokens, out_grad, gate_weight, up_weight, down_weight):
    zl = lax.axis_index("zl")
    xh = lax.axis_index("xh")
    first = zl == 0
    rows, depth = tokens.shape
    ff = gate_weight.shape[1]
    group = 2 * zh_size

    far = pair_swap(jnp.concatenate([gate_weight, up_weight, down_weight], axis=0), zh_size)

    shard = jnp.concatenate([tokens, out_grad], axis=1)
    own = lax.all_to_all(
        jnp.broadcast_to(shard[None], (blocks, rows, 2 * depth)), ("y", "xl"), 0, 0, tiled=True
    )
    own, far = lax.optimization_barrier((own, far))
    own = own.reshape(zh_size // 2, 2, -1, 2 * depth)
    other = swap(own, "c")
    ext = pair_swap(pick(~first, own), zh_size).reshape(-1, 2 * depth)
    ext_other = pair_swap(pick(~first, other), zh_size).reshape(-1, 2 * depth)

    half_tokens = own.size // (2 * depth)
    token_rows = half_tokens // group
    sent_rows = 3 * (ff // LANES) * token_rows
    parts = pl.pallas_call(
        forward_kernel,
        out_shape=jax.ShapeDtypeStruct((group, sent_rows + TAIL, LANES), jnp.float32),
        in_specs=[pl.BlockSpec(memory_space=pltpu.SMEM)]
        + [pl.BlockSpec(memory_space=pltpu.VMEM)] * 8,
        out_specs=pl.BlockSpec(memory_space=pltpu.VMEM),
        compiler_params=pltpu.CompilerParams(vmem_limit_bytes=40 * 2**20),
        cost_estimate=pl.CostEstimate(
            flops=12 * half_tokens * depth * ff,
            bytes_accessed=9 * 2**20,
            transcendentals=0,
        ),
        name="forward_sums",
    )(
        zl.astype(jnp.int32)[None], own, other, ext, ext_other,
        gate_weight, up_weight, down_weight, far,
    )
    parts = lax.all_to_all(parts.astype(jnp.float16), ("zh", "xh"), 0, 0, tiled=True)
    trio = pl.pallas_call(
        middle_kernel,
        out_shape=jax.ShapeDtypeStruct((token_rows, 3 * ff), jnp.bfloat16),
        in_specs=[pl.BlockSpec(memory_space=pltpu.VMEM)],
        out_specs=pl.BlockSpec(memory_space=pltpu.VMEM),
        compiler_params=pltpu.CompilerParams(vmem_limit_bytes=24 * 2**20),
        cost_estimate=pl.CostEstimate(
            flops=8 * group * token_rows * ff,
            bytes_accessed=4 * 2**20,
            transcendentals=token_rows * ff,
        ),
        name="hidden_and_grads",
    )(parts.astype(jnp.float32))

    right, left, beside = [trio], [trio], []
    waiting = [trio]
    for step in range(1, zh_size):
        right.append(turn(right[-1], 2 * zh_size, 1))
        left.append(turn(left[-1], 2 * zh_size, -1))
        waiting = waiting + [right[-1], left[-1]]
        if step >= 3:
            right[-1], left[-1], beside[step - 3] = lax.optimization_barrier(
                (right[-1], left[-1], beside[step - 3])
            )
            waiting = [right[-1], left[-1]]
        beside.append(swap(jnp.concatenate(waiting, axis=0), "xh"))
        waiting = []
    right.append(turn(right[-1], 2 * zh_size, 1))
    beside.append(swap(right[-1], "xh"))

    blocks_in = [trio] + right[1:] + left[1:] + beside
    share = half_tokens
    vmem, hbm = pl.BlockSpec(memory_space=pltpu.VMEM), pl.BlockSpec(memory_space=pltpu.HBM)

    def ordering(width):
        return [
            pltpu.VMEM((2 * share, width), jnp.bfloat16),
            pltpu.SemaphoreType.DMA((4 * zh_size,)),
        ]

    in_own, in_other = pl.pallas_call(
        functools.partial(input_kernel, zh_size),
        out_shape=[
            jax.ShapeDtypeStruct((share, depth), jnp.float32),
            jax.ShapeDtypeStruct((share, depth), jnp.bfloat16),
        ],
        in_specs=[vmem] * 2 + [hbm] * len(blocks_in),
        out_specs=[vmem] * 2,
        scratch_shapes=ordering(2 * ff),
        compiler_params=pltpu.CompilerParams(vmem_limit_bytes=40 * 2**20),
        cost_estimate=pl.CostEstimate(
            flops=8 * share * depth * ff, bytes_accessed=9 * 2**20, transcendentals=0
        ),
        name="input_gradient",
    )(gate_weight, up_weight, *blocks_in)
    in_part = in_own + swap(in_other, "c")
    in_part = lax.all_to_all(
        in_part.astype(jnp.bfloat16).reshape(blocks, rows, depth), ("y", "xl"), 0, 0, tiled=True
    )
    in_grad = jnp.sum(in_part.astype(jnp.float32), axis=0).astype(jnp.bfloat16)

    gate_wgrad, up_wgrad, down_wgrad = pl.pallas_call(
        functools.partial(weight_kernel, zh_size),
        out_shape=[
            jax.ShapeDtypeStruct((depth, ff), jnp.bfloat16),
            jax.ShapeDtypeStruct((depth, ff), jnp.bfloat16),
            jax.ShapeDtypeStruct((ff, depth), jnp.bfloat16),
        ],
        in_specs=[vmem] * 2 + [hbm] * len(blocks_in),
        out_specs=[vmem] * 3,
        scratch_shapes=ordering(3 * ff),
        compiler_params=pltpu.CompilerParams(vmem_limit_bytes=40 * 2**20),
        cost_estimate=pl.CostEstimate(
            flops=12 * share * depth * ff, bytes_accessed=9 * 2**20, transcendentals=0
        ),
        name="weight_gradients",
    )(own, other, *blocks_in)
    return (in_grad, gate_wgrad, up_wgrad, down_wgrad)


def solution(mesh):
    row, col = mesh.devices.shape
    zh_size, y_size = row // 4, col // 4
    fine = Mesh(
        mesh.devices.reshape(zh_size, 2, 2, y_size, 2, 2), ("zh", "zl", "xh", "y", "xl", "c")
    )

    def body(*args):
        return per_device(zh_size, 2 * y_size, *args)

    in_specs = (P(COL, ROW), P(COL, ROW), P(ROW, COL), P(ROW, COL), P(COL, ROW))
    out_specs = (P(COL, ROW), P(ROW, COL), P(ROW, COL), P(COL, ROW))
    return jax.shard_map(
        body, mesh=fine, in_specs=in_specs, out_specs=out_specs, check_vma=False
    )
```
